512 devices in a mesh: dp: 4 (over x), in: 32 (over z, core), out: 4 (over y).
Axes of the slice: x: 4, y: 4, z: 16, core: 2. Of those that a mesh axis runs over, the one named last changes fastest.
Arguments:
- tokens: bfloat16 [512, 8192], P('dp', 'in'), may hold values from -6 to 6
- cotangent: bfloat16 [512, 8192], P('dp', 'in'), may hold values from -3 to 3
- first_blocks: bfloat16 [32, 4, 5, 256, 256], P('in', 'out'), may hold values from -0.15625 to 0.15625
- second_blocks: bfloat16 [32, 4, 5, 256, 256], P('in', 'out'), may hold values from -0.078125 to 0.078125
- first_left: bfloat16 [8192, 512], P('in'), may hold values from -0.0625 to 0.0625
- first_right: bfloat16 [512, 4, 8192], P(None, 'out', 'in'), may hold values from -0.25 to 0.25
- second_left: bfloat16 [4, 8192, 512], P('out', 'in'), may hold values from -0.03125 to 0.03125
- second_right: bfloat16 [512, 8192], P(None, 'in'), may hold values from -0.25 to 0.25
- strides: int32 [4], replicated, may hold values from 1 to 16, as said below
Outputs:
- output: bfloat16 [512, 8192], P('dp', 'in')
- input_grad: bfloat16 [512, 8192], P('dp', 'in')
- first_blocks_grad: float32 [32, 4, 5, 256, 256], P('in', 'out', None, 'dp')
- second_blocks_grad: float32 [32, 4, 5, 256, 256], P('in', 'out', None, 'dp')
- first_left_grad: float32 [8192, 512], P('in', 'dp')
- first_right_grad: float32 [512, 4, 8192], P('dp', 'out', 'in')
- second_left_grad: float32 [4, 8192, 512], P('out', 'in', 'dp')
- second_right_grad: float32 [512, 8192], P('dp', 'in')
The draws below stay inside these ranges and needn't reach their ends.
Inputs may be any that keep to these rules, and one draw needn't show every extreme that they name: strides holds 4 distinct powers of two below 32; 16 is always among them.
All inputs are finite; a program needn't handle non-finite values.
Results may differ from the reference program's by a relative error of at most 0.013.
Values may be sent and summed in bfloat16 or wider, within the bound.
No kernel may reach another device: no remote copies, remote signals or barrier semaphores. Data moves between devices by JAX's collectives and lax.ppermute only.
A program may use at most 64 MiB of HBM per device.

```python
import jax
import jax.numpy as jnp
from jax import lax

D = 8192
FF = 32768
B = 256
LOGRB = 5
RANK = 512
TOK_DEV = 128
RB = 32
PER = 4
KBLOCKS = 5
TOKENS = 512


def draw_strides(key, part):
    order = jax.random.permutation(jax.random.fold_in(key, 11), LOGRB - 1)
    chosen_bits = jnp.concatenate([order[:LOGRB - 2].astype(jnp.int32), jnp.full((1,), LOGRB - 1, jnp.int32)])
    mixed = jax.random.permutation(jax.random.fold_in(key, 12), chosen_bits)
    return jnp.left_shift(jnp.ones_like(mixed), mixed).astype(jnp.int32)


def steps_of(own_key, shape, split, smallest, top_value):
    factor_of, own = 1.0, jax.random.fold_in(own_key, 6)
    for dim, parts in split:
        draws = jnp.exp(jax.random.uniform(jax.random.fold_in(own, dim), (parts,), jnp.float32, smallest / len(split), top_value / len(split)))
        factor_of = factor_of * jnp.repeat(draws, shape[dim] // parts).reshape([-1 if axis == dim else 1 for axis in range(len(shape))])
    return factor_of


def noise(own_key, extent, width, limit, split=(), kind=jnp.bfloat16):
    result = jax.random.normal(own_key, extent, jnp.float32) * width
    if len(split) > 0:
        result = steps_of(own_key, extent, split, -0.22, 0.18) * result
    return jnp.clip(result, min=-limit, max=limit).astype(kind)


def setup_inputs(seed: int = 0) -> dict:
    keys = jax.random.split(jax.random.key(seed), 10)
    tokens = noise(keys[0], (TOKENS, D), 1.0, 6.0, ((0, 4), (1, 32)))
    cotangent = noise(keys[1], (TOKENS, D), 0.5, 3.0, ((0, 4), (1, 32)))
    first_blocks = noise(keys[2], (RB, PER, KBLOCKS, B, B), (KBLOCKS * B) ** -0.5, 0.15625, ((0, 32), (1, 4)))
    second_blocks = noise(keys[3], (RB, PER, KBLOCKS, B, B), (PER * KBLOCKS * B) ** -0.5, 0.078125, ((0, 32), (1, 4)))
    first_left = noise(keys[4], (D, RANK), D ** -0.5, 0.0625, ((0, 32),))
    first_right = noise(keys[5], (RANK, PER, D), RANK ** -0.5, 0.25, ((1, 4), (2, 32)))
    second_left = noise(keys[6], (PER, D, RANK), FF ** -0.5, 0.03125, ((0, 4), (1, 32)))
    second_right = noise(keys[7], (RANK, D), RANK ** -0.5, 0.25, ((1, 32),))
    strides = draw_strides(jax.random.fold_in(keys[9], 71), 0)
    return dict(tokens=tokens, cotangent=cotangent, first_blocks=first_blocks, second_blocks=second_blocks, first_left=first_left, first_right=first_right, second_left=second_left, second_right=second_right, strides=strides)


root_half = 0.7071067811865476
gauss_norm = 0.3989422804014327


def normal_cdf(values):
    return 0.5 * (1.0 + lax.erf(values * root_half))


def reference(tokens, cotangent, first_blocks, second_blocks, first_left, first_right, second_left, second_right, strides):
    token_count = tokens.shape[0]
    stride_all = jnp.concatenate([jnp.zeros((1,), jnp.int32), strides.astype(jnp.int32)])
    block_ids = jnp.arange(RB, dtype=jnp.int32)
    partner = [jnp.bitwise_xor(block_ids, stride_all[stride_index]) for stride_index in range(KBLOCKS)]
    x_blocks = tokens.reshape(token_count, RB, B).astype(jnp.float32)
    dy_blocks = cotangent.reshape(token_count, RB, B).astype(jnp.float32)
    first_full = first_blocks.astype(jnp.float32)
    second_full = second_blocks.astype(jnp.float32)

    latent_in = jnp.dot(tokens, first_left, preferred_element_type=jnp.float32).astype(jnp.bfloat16)
    pre_act = jnp.einsum("tr,rpf->tpf", latent_in.astype(jnp.float32), first_right.astype(jnp.float32))
    pre_act = pre_act.reshape(token_count, PER, RB, B)
    for stride_index in range(KBLOCKS):
        source = jnp.take(x_blocks, partner[stride_index], axis=1)
        weights = jnp.take(first_full[:, :, stride_index], partner[stride_index], axis=0)
        pre_act = pre_act + jnp.einsum("tqb,qpbc->tpqc", source, weights)
    cumul = normal_cdf(pre_act)
    hidden = (pre_act * cumul).astype(jnp.bfloat16)
    hidden_four = hidden.astype(jnp.float32)
    hidden_flat = hidden_four.reshape(token_count, PER, D)
    latent_out = jnp.einsum("tpf,pfr->tr", hidden_flat, second_left.astype(jnp.float32)).astype(jnp.bfloat16)
    out_pre = jnp.dot(latent_out, second_right, preferred_element_type=jnp.float32).reshape(token_count, RB, B)
    for stride_index in range(KBLOCKS):
        source = jnp.take(hidden_four, partner[stride_index], axis=2)
        out_pre = out_pre + jnp.einsum("tprb,rpbc->trc", source, second_full[:, :, stride_index])
    output = out_pre.reshape(token_count, D).astype(jnp.bfloat16)

    cot_latent = jnp.dot(cotangent, second_right.T, preferred_element_type=jnp.float32).astype(jnp.bfloat16)
    hidden_grad = jnp.einsum("tr,pfr->tpf", cot_latent.astype(jnp.float32), second_left.astype(jnp.float32))
    hidden_grad = hidden_grad.reshape(token_count, PER, RB, B)
    for stride_index in range(KBLOCKS):
        source = jnp.take(dy_blocks, partner[stride_index], axis=1)
        weights = jnp.take(second_full[:, :, stride_index], partner[stride_index], axis=0)
        hidden_grad = hidden_grad + jnp.einsum("tqc,qpbc->tpqb", source, weights)
    slope = cumul + pre_act * jnp.exp(-0.5 * pre_act * pre_act) * gauss_norm
    pre_grad = (hidden_grad * slope).astype(jnp.bfloat16)
    grad_four = pre_grad.astype(jnp.float32)
    grad_flat = grad_four.reshape(token_count, PER, D)
    hid_latent = jnp.einsum("tpf,rpf->tr", grad_flat, first_right.astype(jnp.float32)).astype(jnp.bfloat16)
    in_pre = jnp.dot(hid_latent, first_left.T, preferred_element_type=jnp.float32).reshape(token_count, RB, B)
    for stride_index in range(KBLOCKS):
        source = jnp.take(grad_four, partner[stride_index], axis=2)
        in_pre = in_pre + jnp.einsum("tprc,rpbc->trb", source, first_full[:, :, stride_index])
    input_grad = in_pre.reshape(token_count, D).astype(jnp.bfloat16)

    def rounded(value):
        return lax.optimization_barrier(value.astype(jnp.bfloat16)).astype(jnp.float32)

    first_blocks_grad = jnp.zeros(first_blocks.shape, jnp.float32)
    second_blocks_grad = jnp.zeros(second_blocks.shape, jnp.float32)
    first_left_grad = jnp.zeros(first_left.shape, jnp.float32)
    first_right_grad = jnp.zeros(first_right.shape, jnp.float32)
    second_left_grad = jnp.zeros(second_left.shape, jnp.float32)
    second_right_grad = jnp.zeros(second_right.shape, jnp.float32)
    for group_index in range(TOKENS // TOK_DEV):
        low = group_index * TOK_DEV
        high = low + TOK_DEV
        x_group = x_blocks[low:high]
        dy_group = dy_blocks[low:high]
        grad_group = grad_four[low:high]
        hidden_group = hidden_four[low:high]
        first_parts = [jnp.einsum("trb,tprc->rpbc", x_group, jnp.take(grad_group, partner[stride_index], axis=2)) for stride_index in range(KBLOCKS)]
        second_parts = [jnp.einsum("tprb,trc->rpbc", jnp.take(hidden_group, partner[stride_index], axis=2), dy_group) for stride_index in range(KBLOCKS)]
        first_blocks_grad = first_blocks_grad + rounded(jnp.stack(first_parts, axis=2))
        second_blocks_grad = second_blocks_grad + rounded(jnp.stack(second_parts, axis=2))
        first_left_grad = first_left_grad + jnp.dot(tokens[low:high].T, hid_latent[low:high], preferred_element_type=jnp.float32)
        first_right_grad = first_right_grad + jnp.einsum("tr,tpf->rpf", latent_in[low:high].astype(jnp.float32), grad_flat[low:high])
        second_left_grad = second_left_grad + jnp.einsum("tpf,tr->pfr", hidden_flat[low:high], cot_latent[low:high].astype(jnp.float32))
        second_right_grad = second_right_grad + jnp.dot(latent_out[low:high].T, cotangent[low:high], preferred_element_type=jnp.float32)
    return (output, input_grad, first_blocks_grad, second_blocks_grad, first_left_grad, first_right_grad, second_left_grad, second_right_grad)
```

```python
import jax
import jax.numpy as jnp
from jax import lax
from jax.sharding import PartitionSpec as P

root_half = 0.7071067811865476
gauss_norm = 0.3989422804014327
f32 = jnp.float32
bf16 = jnp.bfloat16
BITS = 5


def normal_cdf(values):
    return 0.5 * (1.0 + lax.erf(values * root_half))


def swap_bit(block, bit):
    count = lax.axis_size("in")
    return lax.ppermute(block, "in", [(i, i ^ (1 << bit)) for i in range(count)])


def ring(block, axis, distance):
    count = lax.axis_size(axis)
    return lax.ppermute(block, axis, [(i, (i + distance) % count) for i in range(count)])


def dot(a, b, ca, cb):
    return lax.dot_general(a, b, (((ca,), (cb,)), ((), ())), preferred_element_type=f32)


def pick(stack, index):
    return lax.dynamic_index_in_dim(stack, index, 0, keepdims=False)


def sum_rows(partial, axes):
    group, width = partial.shape
    sent = partial.astype(bf16).reshape(group, width // 128, 128)
    got = lax.all_to_all(sent, axes, 0, 0, tiled=True)
    return jnp.sum(got.astype(f32), axis=0).astype(bf16)


def spread_rows(row, axes, group):
    sent = jnp.broadcast_to(row[None], (group,) + row.shape)
    got = lax.all_to_all(sent, axes, 0, 0, tiled=True)
    return got.reshape(group, row.shape[0] * row.shape[1])


def scatter_dp(parts):
    me = lax.axis_index("dp")
    count = lax.axis_size("dp")
    sent = parts.astype(bf16)
    total = pick(sent, me).astype(f32)
    for distance in range(1, count):
        got = ring(pick(sent, (me + distance) % count), "dp", distance)
        total = total + got.astype(f32)
    return total


def per_device(
    tokens,
    cotangent,
    first_blocks,
    second_blocks,
    first_left,
    first_right,
    second_left,
    second_right,
    strides,
):
    count = tokens.shape[0]
    size = tokens.shape[1]
    rank = first_left.shape[1]
    n_in = lax.axis_size("in")
    n_out = lax.axis_size("out")
    n_dp = lax.axis_size("dp")
    p = lax.axis_index("out")
    w1 = first_blocks[0, 0]
    w2 = second_blocks[0, 0]
    right1 = first_right[:, 0]
    left2 = second_left[0]
    all_axes = ("out", "in")
    group = n_in * n_out
    kcount = w1.shape[0]
    powers = jnp.left_shift(1, jnp.arange(BITS, dtype=jnp.int32))
    match = strides[None, :] == powers[:, None]
    present = jnp.any(match, axis=1)
    k_of_bit = jnp.argmax(match, axis=1) + 1
    bit_of_k = jnp.argmax(match, axis=0)

    first = jnp.einsum("tb,kbc->ktc", tokens, w1, preferred_element_type=f32)
    second = jnp.einsum("tc,kbc->ktb", cotangent, w2, preferred_element_type=f32)
    both = jnp.stack([first, second], axis=1).astype(bf16)
    arrived = [swap_bit(pick(both, k_of_bit[b]), b) for b in range(BITS)]

    share = count // n_out
    x_share = lax.dynamic_slice_in_dim(tokens, p * share, share, 0)
    dy_share = lax.dynamic_slice_in_dim(cotangent, p * share, share, 0)
    part = jnp.concatenate([dot(x_share, first_left, 1, 0), dot(dy_share, second_right, 1, 1)], axis=1)
    latent = spread_rows(sum_rows(part, "in"), all_axes, group)
    a, e = latent[:, :rank], latent[:, rank:]

    z = first[0] + dot(a, right1, 1, 0)
    g = second[0] + dot(e, left2, 1, 1)
    for b in range(BITS):
        got = arrived[b].astype(f32)
        z = z + jnp.where(present[b], got[0], 0.0)
        g = g + jnp.where(present[b], got[1], 0.0)
    cumul = normal_cdf(z)
    h = (z * cumul).astype(bf16)
    slope = cumul + z * jnp.exp(-0.5 * z * z) * gauss_norm
    dz = (g * slope).astype(bf16)

    hd = jnp.stack([h, dz])
    near_bits = jnp.stack([swap_bit(hd, b) for b in range(BITS)])
    near = [hd] + [pick(near_bits, bit_of_k[k]) for k in range(kcount - 1)]

    part = jnp.concatenate([dot(h, left2, 1, 0), dot(dz, right1, 1, 1)], axis=1)
    row = sum_rows(part, all_axes)

    hn = jnp.stack([n[0] for n in near])
    dn = jnp.stack([n[1] for n in near])
    block_out = jnp.einsum("ktb,kbc->tc", hn, w2, preferred_element_type=f32)
    block_in = jnp.einsum("ktc,kbc->tb", dn, w1, preferred_element_type=f32)
    blocks = jnp.stack([block_out, block_in])
    blocks_sent = blocks.astype(bf16)
    for distance in range(1, n_out):
        blocks = blocks + ring(blocks_sent, "out", distance).astype(f32)

    grad1 = jnp.einsum("tb,ktc->kbc", tokens, dn, preferred_element_type=f32)
    grad2 = jnp.einsum("ktb,tc->kbc", hn, cotangent, preferred_element_type=f32)

    def by_dp(grad):
        rows = size // n_dp
        cut = grad.reshape(kcount, n_dp, rows, size)
        return jnp.swapaxes(cut, 0, 1).reshape(n_dp, kcount * rows, size)

    right1_part = dot(a, dz, 0, 0).reshape(n_dp, rank // n_dp, size)
    left2_part = dot(e, h, 0, 0).reshape(n_dp, rank // n_dp, size)
    done = scatter_dp(jnp.concatenate([by_dp(grad1), by_dp(grad2), right1_part, left2_part], axis=1))
    rows = kcount * size // n_dp
    first_blocks_grad = done[:rows].reshape(1, 1, kcount, size // n_dp, size)
    second_blocks_grad = done[rows : 2 * rows].reshape(1, 1, kcount, size // n_dp, size)
    first_right_grad = done[2 * rows : 2 * rows + rank // n_dp][:, None]
    second_left_grad = done[2 * rows + rank // n_dp :].T[None]

    latent = spread_rows(row, all_axes, group)
    c, f = latent[:, :rank], latent[:, rank:]
    output = (blocks[0] + dot(c, second_right, 1, 0)).astype(bf16)
    input_grad = (blocks[1] + dot(f, first_left, 1, 1)).astype(bf16)
    left1_part = dot(f, tokens, 0, 0).reshape(n_dp, rank // n_dp, size)
    right2_part = dot(c, cotangent, 0, 0).reshape(n_dp, rank // n_dp, size)
    sent = jnp.concatenate([left1_part, right2_part], axis=1).astype(bf16)
    got = lax.all_to_all(sent, "dp", 0, 0, tiled=True)
    late = jnp.sum(got.astype(f32), axis=0)
    first_left_grad = late[: rank // n_dp].T
    second_right_grad = late[rank // n_dp :]
    return (
        output,
        input_grad,
        first_blocks_grad,
        second_blocks_grad,
        first_left_grad,
        first_right_grad,
        second_left_grad,
        second_right_grad,
    )


def solution(mesh):
    in_specs = (
        P("dp", "in"),
        P("dp", "in"),
        P("in", "out", None, None, None),
        P("in", "out", None, None, None),
        P("in", None),
        P(None, "out", "in"),
        P("out", "in", None),
        P(None, "in"),
        P(),
    )
    out_specs = (
        P("dp", "in"),
        P("dp", "in"),
        P("in", "out", None, "dp", None),
        P("in", "out", None, "dp", None),
        P("in", "dp"),
        P("dp", "out", "in"),
        P("out", "in", "dp"),
        P("dp", "in"),
    )
    return jax.shard_map(
        per_device, mesh=mesh, in_specs=in_specs, out_specs=out_specs, check_vma=False
    )
```

```python
from functools import partial

import jax
import jax.numpy as jnp
from jax import lax
from jax.experimental import pallas as pl
from jax.experimental.pallas import tpu as pltpu
from jax.sharding import PartitionSpec as P

root_half = 0.7071067811865476
gauss_norm = 0.3989422804014327
f32 = jnp.float32
bf16 = jnp.bfloat16
BITS = 5
SLOTS = 5
FIRST = (4, 3)
FIRST_A = (4, 3)
LONG = 20 * 10**9
VMEM_LIMIT = 60 * 2**20
VM = pl.BlockSpec(memory_space=pltpu.VMEM)
SM = pl.BlockSpec(memory_space=pltpu.SMEM)


def swap_bit(block, bit):
    count = lax.axis_size("in")
    return lax.ppermute(block, "in", [(i, i ^ (1 << bit)) for i in range(count)])


def dot(a, b, ca, cb):
    return lax.dot_general(a, b, (((ca,), (cb,)), ((), ())), preferred_element_type=f32)


def exchange(parts, axes):
    return lax.all_to_all(parts, axes, 0, 0, tiled=True)


def spread(row, axes, group):
    return exchange(jnp.broadcast_to(row[None], (group,) + row.shape), axes)


def ring(block, axis, distance):
    count = lax.axis_size(axis)
    return lax.ppermute(block, axis, [(i, (i + distance) % count) for i in range(count)])


def pick(stack, index):
    return lax.dynamic_index_in_dim(stack, index, 0, keepdims=False)


def together(*values):
    return lax.optimization_barrier(values)


def kernel_call(body, specs, shapes, flops, name, after=None):
    tokens = [] if after is None else [after]
    call = pl.pallas_call(
        lambda *refs: body(*refs[len(tokens) :]),
        in_specs=[pl.BlockSpec(memory_space=pl.ANY)] * len(tokens) + specs,
        out_specs=[VM] * len(shapes),
        out_shape=[jax.ShapeDtypeStruct(s, d) for s, d in shapes],
        compiler_params=pltpu.CompilerParams(vmem_limit_bytes=VMEM_LIMIT),
        cost_estimate=pl.CostEstimate(flops=flops, bytes_accessed=4 * 2**20, transcendentals=0),
        name=name,
    )
    return lambda *values: call(*tokens, *values)


def gate(value, after=None):
    tokens = [] if after is None else [after]
    return pl.pallas_call(
        lambda *refs: None,
        in_specs=[pl.BlockSpec(memory_space=pl.ANY)] * (1 + len(tokens)),
        out_specs=pl.BlockSpec(memory_space=pl.ANY),
        out_shape=jax.ShapeDtypeStruct(value.shape, value.dtype),
        input_output_aliases={0: 0},
        cost_estimate=pl.CostEstimate(flops=LONG, bytes_accessed=2**20, transcendentals=0),
        name="gate",
    )(value, *tokens)


def slot_of_bit(strides_ref, bit):
    slot = 0
    for k in range(SLOTS - 1):
        slot = slot + jnp.where(strides_ref[k] == 1 << bit, k + 1, 0)
    return slot


def products(bits, strides_ref, x_ref, dy_ref, w1_ref, w2_ref, *send_refs):
    x, dy = x_ref[...], dy_ref[...]
    for bit, send_ref in zip(bits, send_refs):
        slot = slot_of_bit(strides_ref, bit)
        send_ref[0] = dot(x, w1_ref[slot], 1, 0).astype(bf16)
        send_ref[1] = dot(dy, w2_ref[slot], 1, 1).astype(bf16)


def sum_products(x_ref, dy_ref, w1_ref, w2_ref, *refs):
    got, total_ref = refs[:-1], refs[-1]
    own = (dot(x_ref[...], w1_ref[0], 1, 0), dot(dy_ref[...], w2_ref[0], 1, 1))
    for half in range(2):
        value = own[half]
        for ref in got:
            value = value + ref[half].astype(f32)
        total_ref[half] = value


def activations(base_ref, latent_ref, right1_ref, left2_ref, *refs):
    hd_refs, part_ref = refs[:3], refs[3]
    rank = right1_ref.shape[0]
    right1, left2 = right1_ref[...], left2_ref[...]
    z = base_ref[0] + dot(latent_ref[:, :rank], right1, 1, 0)
    g = base_ref[1] + dot(latent_ref[:, rank:], left2, 1, 1)
    cumul = 0.5 * (1.0 + lax.erf(z * root_half))
    slope = cumul + z * jnp.exp(-0.5 * z * z) * gauss_norm
    h = (z * cumul).astype(bf16)
    dz = (g * slope).astype(bf16)
    for hd_ref in hd_refs:
        hd_ref[0] = h
        hd_ref[1] = dz
    part_ref[:, :rank] = dot(h, left2, 1, 0).astype(bf16)
    part_ref[:, rank:] = dot(dz, right1, 1, 1).astype(bf16)


def block_outputs(bits, strides_ref, w1_ref, w2_ref, hd_ref, *refs):
    near, out_ref = refs[:-1], refs[-1]
    size = w1_ref.shape[1]
    block_out = dot(hd_ref[0], w2_ref[0], 1, 0)
    block_in = dot(hd_ref[1], w1_ref[0], 1, 1)
    for bit, ref in zip(bits, near):
        slot = slot_of_bit(strides_ref, bit)
        block_out = block_out + dot(ref[0], w2_ref[slot], 1, 0)
        block_in = block_in + dot(ref[1], w1_ref[slot], 1, 1)
    out_ref[:, :size] = block_out.astype(bf16)
    out_ref[:, size:] = block_in.astype(bf16)


def block_grads(bits, strides_ref, x_ref, dy_ref, latent_ref, hd_ref, *refs):
    near, out_ref = refs[:-1], refs[-1]
    size = x_ref.shape[1]
    rank = latent_ref.shape[1] // 2
    parts = out_ref.shape[0]
    rows = size // parts
    x, dy = x_ref[...], dy_ref[...]

    def store(slot, ref):
        grad1, grad2 = dot(x, ref[1], 0, 0), dot(ref[0], dy, 0, 0)
        for d in range(parts):
            own = slice(d * rows, (d + 1) * rows)
            start = pl.multiple_of(slot * rows, rows)
            out_ref[d, pl.ds(start, rows), :] = grad1[own].astype(bf16)
            start = pl.multiple_of((slot + SLOTS) * rows, rows)
            out_ref[d, pl.ds(start, rows), :] = grad2[own].astype(bf16)

    store(0, hd_ref)
    for bit, ref in zip(bits, near):
        store(slot_of_bit(strides_ref, bit), ref)
    first = 2 * SLOTS * rows
    take = rank // parts
    for d in range(parts):
        right1 = dot(latent_ref[:, d * take : (d + 1) * take], hd_ref[1], 0, 0)
        left2 = dot(latent_ref[:, rank + d * take : rank + (d + 1) * take], hd_ref[0], 0, 0)
        out_ref[d, first : first + take, :] = right1.astype(bf16)
        out_ref[d, first + take : first + 2 * take, :] = left2.astype(bf16)


def sum_grads(*refs):
    got, (first_ref, second_ref, right1_ref, left2_ref) = refs[:-4], refs[-4:]
    rows = first_ref.shape[0]
    take = right1_ref.shape[0]

    def total(low, high):
        value = got[0][low:high, :].astype(f32)
        for ref in got[1:]:
            value = value + ref[low:high, :].astype(f32)
        return value

    first_ref[...] = total(0, rows)
    second_ref[...] = total(rows, 2 * rows)
    right1_ref[...] = total(2 * rows, 2 * rows + take)
    left2_ref[...] = total(2 * rows + take, 2 * rows + 2 * take).T


def for_bits(
    bits,
    tokens,
    cotangent,
    first_blocks,
    second_blocks,
    first_left,
    first_right,
    second_left,
    second_right,
    strides,
):
    count, size = tokens.shape
    rank = first_left.shape[1]
    n_in = lax.axis_size("in")
    n_out = lax.axis_size("out")
    n_dp = lax.axis_size("dp")
    p = lax.axis_index("out")
    w1 = first_blocks[0, 0]
    w2 = second_blocks[0, 0]
    right1 = first_right[:, 0]
    left2 = second_left[0]
    share = count // n_out
    wide = 2 * rank
    tile = (wide // 128, 128)
    flops = 2 * count * size * size
    pair = ((2, count, size), bf16)

    x_share = lax.dynamic_slice_in_dim(tokens, p * share, share, 0)
    dy_share = lax.dynamic_slice_in_dim(cotangent, p * share, share, 0)
    part = jnp.concatenate([dot(x_share, first_left, 1, 0), dot(dy_share, second_right, 1, 1)], axis=1)
    got = exchange(part.astype(bf16).reshape((share,) + tile), "in")

    def sent(some, after):
        sends = kernel_call(
            partial(products, some), [SM, VM, VM, VM, VM], [pair] * len(some), LONG, "products", after
        )(strides, tokens, cotangent, w1, w2)
        return [swap_bit(send, bit) for send, bit in zip(sends, some)]

    arrived = sent([b for b in bits if b in FIRST_A], None)
    row = jnp.sum(got.astype(f32), axis=0).astype(bf16)
    arrived += sent([b for b in bits if b not in FIRST_A], row)
    (base,) = kernel_call(
        sum_products, [VM] * (4 + len(bits)), [((2, count, size), f32)], LONG, "sum_products"
    )(tokens, cotangent, w1, w2, *arrived)
    mine = spread(row, "in", n_in)
    latent = spread(gate(mine), "out", n_out).reshape(count, wide)

    hd, first_hd, second_hd, part = kernel_call(
        activations, [VM] * 4, [pair] * 3 + [((count, wide), bf16)], 16 * flops, "activations"
    )(base, latent, right1, left2)

    got = exchange(part.reshape(n_out, share, wide), "out")
    first_hd = gate(first_hd)
    part = jnp.sum(got.astype(f32), axis=0).astype(bf16)
    second_hd = gate(second_hd, part)
    near = [swap_bit(first_hd if bit in FIRST else second_hd, bit) for bit in bits]
    got = exchange(part.reshape((share,) + tile), "in")
    row = jnp.sum(got.astype(f32), axis=0).astype(bf16)
    (blocks,) = kernel_call(
        partial(block_outputs, bits), [SM] + [VM] * (3 + len(bits)), [((count, 2 * size), bf16)], LONG, "block_outputs", row
    )(strides, w1, w2, hd, *near)

    rows = SLOTS * size // n_dp
    take = rank // n_dp
    (grads,) = kernel_call(
        partial(block_grads, bits),
        [SM] + [VM] * (4 + len(bits)),
        [((n_dp, 2 * (rows + take), size), bf16)],
        LONG,
        "block_grads",
        row,
    )(strides, tokens, cotangent, latent, hd, *near)
    mine = spread(row, "in", n_in).reshape(share, wide)
    me = lax.axis_index("dp")
    grads = [pick(grads, me)] + [ring(pick(grads, (me + d) % n_dp), "dp", d) for d in range(1, n_dp)]
    both = jnp.concatenate([mine.reshape(share * wide // 256, 256), blocks.reshape(count * 2 * size // 256, 256)])
    both = spread(gate(both), "out", n_out)
    cut = share * wide // 256
    cf = both[:, :cut].reshape(count, wide)
    blocks = jnp.sum(both[:, cut:].astype(f32), axis=0).reshape(count, 2 * size)
    c, f = cf[:, :rank], cf[:, rank:]
    parts = jnp.concatenate(
        [dot(f, tokens, 0, 0).reshape(n_dp, take, size), dot(c, cotangent, 0, 0).reshape(n_dp, take, size)], axis=1
    ).astype(bf16)
    first_grad, second_grad, right1_grad, left2_grad = kernel_call(
        sum_grads,
        [VM] * n_dp,
        [((rows, size), f32), ((rows, size), f32), ((take, size), f32), ((size, take), f32)],
        LONG,
        "sum_grads",
    )(*grads)
    parts, first_grad, second_grad, right1_grad, left2_grad = together(
        parts, first_grad, second_grad, right1_grad, left2_grad
    )
    parts = exchange(parts, "dp")
    output = (blocks[:, :size] + dot(c, second_right, 1, 0)).astype(bf16)
    input_grad = (blocks[:, size:] + dot(f, first_left, 1, 1)).astype(bf16)
    late = jnp.sum(parts.astype(f32), axis=0)
    left1_grad, right2_grad = late[:take].T, late[take:]
    block_shape = (1, 1, SLOTS, size // n_dp, size)
    return (
        output,
        input_grad,
        first_grad.reshape(block_shape),
        second_grad.reshape(block_shape),
        left1_grad,
        right1_grad[:, None],
        left2_grad[None],
        right2_grad,
    )


def per_device(*args):
    absent = (1 << BITS) - 1 - jnp.sum(args[-1])
    index = sum((absent >= (1 << b)).astype(jnp.int32) for b in range(1, BITS - 1))
    cases = [tuple(b for b in range(BITS) if b != gone) for gone in range(BITS - 1)]
    return lax.switch(index, [partial(for_bits, bits) for bits in cases], *args)


def solution(mesh):
    in_specs = (
        P("dp", "in"),
        P("dp", "in"),
        P("in", "out", None, None, None),
        P("in", "out", None, None, None),
        P("in", None),
        P(None, "out", "in"),
        P("out", "in", None),
        P(None, "in"),
        P(),
    )
    out_specs = (
        P("dp", "in"),
        P("dp", "in"),
        P("in", "out", None, "dp", None),
        P("in", "out", None, "dp", None),
        P("in", "dp"),
        P("dp", "out", "in"),
        P("out", "in", "dp"),
        P("dp", "in"),
    )
    return jax.shard_map(
        per_device, mesh=mesh, in_specs=in_specs, out_specs=out_specs, check_vma=False
    )
```

```python
from functools import partial

import jax
import jax.numpy as jnp
from jax import lax
from jax.experimental import pallas as pl
from jax.experimental.pallas import tpu as pltpu
from jax.sharding import PartitionSpec as P

root_half = 0.7071067811865476
gauss_norm = 0.3989422804014327
f32 = jnp.float32
bf16 = jnp.bfloat16
BITS = 5
SLOTS = 5
FIRST = (4,)
FIRST_A = (4,)
LONG = 20 * 10**9
VMEM_LIMIT = 60 * 2**20
VM = pl.BlockSpec(memory_space=pltpu.VMEM)
SM = pl.BlockSpec(memory_space=pltpu.SMEM)


def swap_bit(block, bit):
    count = lax.axis_size("in")
    return lax.ppermute(block, "in", [(i, i ^ (1 << bit)) for i in range(count)])


def dot(a, b, ca, cb):
    return lax.dot_general(a, b, (((ca,), (cb,)), ((), ())), preferred_element_type=f32)


def exchange(parts, axes):
    return lax.all_to_all(parts, axes, 0, 0, tiled=True)


def spread(row, axes, group):
    return exchange(jnp.broadcast_to(row[None], (group,) + row.shape), axes)


def ring(block, axis, distance):
    count = lax.axis_size(axis)
    return lax.ppermute(block, axis, [(i, (i + distance) % count) for i in range(count)])


def pick(stack, index):
    return lax.dynamic_index_in_dim(stack, index, 0, keepdims=False)


def together(*values):
    return lax.optimization_barrier(values)


def kernel_call(body, specs, shapes, flops, name, after=None):
    tokens = [] if after is None else [after]
    call = pl.pallas_call(
        lambda *refs: body(*refs[len(tokens) :]),
        in_specs=[pl.BlockSpec(memory_space=pl.ANY)] * len(tokens) + specs,
        out_specs=[VM] * len(shapes),
        out_shape=[jax.ShapeDtypeStruct(s, d) for s, d in shapes],
        compiler_params=pltpu.CompilerParams(vmem_limit_bytes=VMEM_LIMIT),
        cost_estimate=pl.CostEstimate(flops=flops, bytes_accessed=4 * 2**20, transcendentals=0),
        name=name,
    )
    return lambda *values: call(*tokens, *values)


def gate(value, *tokens):
    return pl.pallas_call(
        lambda *refs: None,
        in_specs=[pl.BlockSpec(memory_space=pl.ANY)] * (1 + len(tokens)),
        out_specs=pl.BlockSpec(memory_space=pl.ANY),
        out_shape=jax.ShapeDtypeStruct(value.shape, value.dtype),
        input_output_aliases={0: 0},
        cost_estimate=pl.CostEstimate(flops=LONG, bytes_accessed=2**20, transcendentals=0),
        name="gate",
    )(value, *tokens)


def slot_of_bit(strides_ref, bit):
    slot = 0
    for k in range(SLOTS - 1):
        slot = slot + jnp.where(strides_ref[k] == 1 << bit, k + 1, 0)
    return slot


def products(bits, strides_ref, x_ref, dy_ref, w1_ref, w2_ref, *send_refs):
    x, dy = x_ref[...], dy_ref[...]
    for bit, send_ref in zip(bits, send_refs):
        slot = slot_of_bit(strides_ref, bit)
        send_ref[0] = dot(x, w1_ref[slot], 1, 0).astype(bf16)
        send_ref[1] = dot(dy, w2_ref[slot], 1, 1).astype(bf16)


def sum_products(x_ref, dy_ref, w1_ref, w2_ref, *refs):
    got, total_ref = refs[:-1], refs[-1]
    own = (dot(x_ref[...], w1_ref[0], 1, 0), dot(dy_ref[...], w2_ref[0], 1, 1))
    for half in range(2):
        value = own[half]
        for ref in got:
            value = value + ref[half].astype(f32)
        total_ref[half] = value


def activations(base_ref, latent_ref, right1_ref, left2_ref, *refs):
    hd_refs, part_ref = refs[:3], refs[3]
    rank = right1_ref.shape[0]
    right1, left2 = right1_ref[...], left2_ref[...]
    z = base_ref[0] + dot(latent_ref[:, :rank], right1, 1, 0)
    g = base_ref[1] + dot(latent_ref[:, rank:], left2, 1, 1)
    cumul = 0.5 * (1.0 + lax.erf(z * root_half))
    slope = cumul + z * jnp.exp(-0.5 * z * z) * gauss_norm
    h = (z * cumul).astype(bf16)
    dz = (g * slope).astype(bf16)
    for hd_ref in hd_refs:
        hd_ref[0] = h
        hd_ref[1] = dz
    part_ref[:, :rank] = dot(h, left2, 1, 0).astype(bf16)
    part_ref[:, rank:] = dot(dz, right1, 1, 1).astype(bf16)


def block_outputs(bits, strides_ref, w1_ref, w2_ref, hd_ref, *refs):
    near, out_ref = refs[:-1], refs[-1]
    size = w1_ref.shape[1]
    block_out = dot(hd_ref[0], w2_ref[0], 1, 0)
    block_in = dot(hd_ref[1], w1_ref[0], 1, 1)
    for bit, ref in zip(bits, near):
        slot = slot_of_bit(strides_ref, bit)
        block_out = block_out + dot(ref[0], w2_ref[slot], 1, 0)
        block_in = block_in + dot(ref[1], w1_ref[slot], 1, 1)
    out_ref[:, :size] = block_out.astype(bf16)
    out_ref[:, size:] = block_in.astype(bf16)


def block_grads(bits, strides_ref, x_ref, dy_ref, latent_ref, hd_ref, *refs):
    near, out_ref = refs[:-1], refs[-1]
    size = x_ref.shape[1]
    rank = latent_ref.shape[1] // 2
    parts = out_ref.shape[0]
    rows = size // parts
    x, dy = x_ref[...], dy_ref[...]

    def store(slot, ref):
        grad1, grad2 = dot(x, ref[1], 0, 0), dot(ref[0], dy, 0, 0)
        for d in range(parts):
            own = slice(d * rows, (d + 1) * rows)
            start = pl.multiple_of(slot * rows, rows)
            out_ref[d, pl.ds(start, rows), :] = grad1[own].astype(bf16)
            start = pl.multiple_of((slot + SLOTS) * rows, rows)
            out_ref[d, pl.ds(start, rows), :] = grad2[own].astype(bf16)

    store(0, hd_ref)
    for bit, ref in zip(bits, near):
        store(slot_of_bit(strides_ref, bit), ref)
    first = 2 * SLOTS * rows
    take = rank // parts
    for d in range(parts):
        right1 = dot(latent_ref[:, d * take : (d + 1) * take], hd_ref[1], 0, 0)
        left2 = dot(latent_ref[:, rank + d * take : rank + (d + 1) * take], hd_ref[0], 0, 0)
        out_ref[d, first : first + take, :] = right1.astype(bf16)
        out_ref[d, first + take : first + 2 * take, :] = left2.astype(bf16)


def sum_grads(*refs):
    got, (first_ref, second_ref, right1_ref, left2_ref) = refs[:-4], refs[-4:]
    rows = first_ref.shape[0]
    take = right1_ref.shape[0]

    def total(low, high):
        value = got[0][low:high, :].astype(f32)
        for ref in got[1:]:
            value = value + ref[low:high, :].astype(f32)
        return value

    first_ref[...] = total(0, rows)
    second_ref[...] = total(rows, 2 * rows)
    right1_ref[...] = total(2 * rows, 2 * rows + take)
    left2_ref[...] = total(2 * rows + take, 2 * rows + 2 * take).T


def for_bits(
    bits,
    tokens,
    cotangent,
    first_blocks,
    second_blocks,
    first_left,
    first_right,
    second_left,
    second_right,
    strides,
):
    count, size = tokens.shape
    rank = first_left.shape[1]
    n_in = lax.axis_size("in")
    n_out = lax.axis_size("out")
    n_dp = lax.axis_size("dp")
    p = lax.axis_index("out")
    w1 = first_blocks[0, 0]
    w2 = second_blocks[0, 0]
    right1 = first_right[:, 0]
    left2 = second_left[0]
    share = count // n_out
    wide = 2 * rank
    tile = (wide // 128, 128)
    flops = 2 * count * size * size
    pair = ((2, count, size), bf16)

    x_share = lax.dynamic_slice_in_dim(tokens, p * share, share, 0)
    dy_share = lax.dynamic_slice_in_dim(cotangent, p * share, share, 0)
    part = jnp.concatenate([dot(x_share, first_left, 1, 0), dot(dy_share, second_right, 1, 1)], axis=1)
    got = exchange(part.astype(bf16).reshape((share,) + tile), "in")

    def sent(some, after):
        sends = kernel_call(
            partial(products, some), [SM, VM, VM, VM, VM], [pair] * len(some), LONG, "products", after
        )(strides, tokens, cotangent, w1, w2)
        return [swap_bit(send, bit) for send, bit in zip(sends, some)]

    arrived = sent([b for b in bits if b in FIRST_A], None)
    row = jnp.sum(got.astype(f32), axis=0).astype(bf16)
    arrived += sent([b for b in bits if b not in FIRST_A], row)
    (base,) = kernel_call(
        sum_products, [VM] * (4 + len(bits)), [((2, count, size), f32)], LONG, "sum_products"
    )(tokens, cotangent, w1, w2, *arrived)
    mine = spread(row, "in", n_in)
    latent = spread(gate(mine), "out", n_out).reshape(count, wide)

    hd, first_hd, second_hd, part = kernel_call(
        activations, [VM] * 4, [pair] * 3 + [((count, wide), bf16)], 16 * flops, "activations"
    )(base, latent, right1, left2)

    got = exchange(part.reshape(n_out, share, wide), "out")
    first_hd = gate(first_hd)
    part = jnp.sum(got.astype(f32), axis=0).astype(bf16)
    second_hd = gate(second_hd, part)
    near = [swap_bit(first_hd if bit in FIRST else second_hd, bit) for bit in bits]
    got = exchange(part.reshape((share,) + tile), "in")
    row = jnp.sum(got.astype(f32), axis=0).astype(bf16)
    (blocks,) = kernel_call(
        partial(block_outputs, bits), [SM] + [VM] * (3 + len(bits)), [((count, 2 * size), bf16)], LONG, "block_outputs", row
    )(strides, w1, w2, hd, *near)

    rows = SLOTS * size // n_dp
    take = rank // n_dp
    (grads,) = kernel_call(
        partial(block_grads, bits),
        [SM] + [VM] * (4 + len(bits)),
        [((n_dp, 2 * (rows + take), size), bf16)],
        LONG,
        "block_grads",
        row,
    )(strides, tokens, cotangent, latent, hd, *near)
    mine = spread(row, "in", n_in).reshape(share, wide)
    me = lax.axis_index("dp")
    sums = [pick(grads, me)] + [ring(pick(grads, (me + d) % n_dp), "dp", d) for d in range(1, n_dp)]
    both = jnp.concatenate([mine.reshape(share * wide // 256, 256), blocks.reshape(count * 2 * size // 256, 256)])
    both = spread(gate(both, grads), "out", n_out)
    cut = share * wide // 256
    cf = both[:, :cut].reshape(count, wide)
    blocks = jnp.sum(both[:, cut:].astype(f32), axis=0).reshape(count, 2 * size)
    c, f = cf[:, :rank], cf[:, rank:]
    parts = jnp.concatenate(
        [dot(f, tokens, 0, 0).reshape(n_dp, take, size), dot(c, cotangent, 0, 0).reshape(n_dp, take, size)], axis=1
    ).astype(bf16)
    sums[0] = gate(sums[0], *sums[1:])
    parts, sums[0] = together(parts, sums[0])
    first_grad, second_grad, right1_grad, left2_grad = kernel_call(
        sum_grads,
        [VM] * n_dp,
        [((rows, size), f32), ((rows, size), f32), ((take, size), f32), ((size, take), f32)],
        LONG,
        "sum_grads",
        parts,
    )(*sums)
    parts = exchange(parts, "dp")
    output = (blocks[:, :size] + dot(c, second_right, 1, 0)).astype(bf16)
    input_grad = (blocks[:, size:] + dot(f, first_left, 1, 1)).astype(bf16)
    late = jnp.sum(parts.astype(f32), axis=0)
    left1_grad, right2_grad = late[:take].T, late[take:]
    block_shape = (1, 1, SLOTS, size // n_dp, size)
    return (
        output,
        input_grad,
        first_grad.reshape(block_shape),
        second_grad.reshape(block_shape),
        left1_grad,
        right1_grad[:, None],
        left2_grad[None],
        right2_grad,
    )


def per_device(*args):
    absent = (1 << BITS) - 1 - jnp.sum(args[-1])
    index = sum((absent >= (1 << b)).astype(jnp.int32) for b in range(1, BITS - 1))
    cases = [tuple(b for b in range(BITS) if b != gone) for gone in range(BITS - 1)]
    return lax.switch(index, [partial(for_bits, bits) for bits in cases], *args)


def solution(mesh):
    in_specs = (
        P("dp", "in"),
        P("dp", "in"),
        P("in", "out", None, None, None),
        P("in", "out", None, None, None),
        P("in", None),
        P(None, "out", "in"),
        P("out", "in", None),
        P(None, "in"),
        P(),
    )
    out_specs = (
        P("dp", "in"),
        P("dp", "in"),
        P("in", "out", None, "dp", None),
        P("in", "out", None, "dp", None),
        P("in", "dp"),
        P("dp", "out", "in"),
        P("out", "in", "dp"),
        P("dp", "in"),
    )
    return jax.shard_map(
        per_device, mesh=mesh, in_specs=in_specs, out_specs=out_specs, check_vma=False
    )
```

```python
from functools import partial

import jax
import jax.numpy as jnp
from jax import lax
from jax.experimental import pallas as pl
from jax.experimental.pallas import tpu as pltpu
from jax.sharding import PartitionSpec as P

root_half = 0.7071067811865476
gauss_norm = 0.3989422804014327
f32 = jnp.float32
bf16 = jnp.bfloat16
BITS = 5
SLOTS = 5
FIRST = (4,)
FIRST_A = (4,)
LONG = 20 * 10**9
VMEM_LIMIT = 60 * 2**20
VM = pl.BlockSpec(memory_space=pltpu.VMEM)
SM = pl.BlockSpec(memory_space=pltpu.SMEM)


def swap_bit(block, bit):
    count = lax.axis_size("in")
    return lax.ppermute(block, "in", [(i, i ^ (1 << bit)) for i in range(count)])


def dot(a, b, ca, cb):
    return lax.dot_general(a, b, (((ca,), (cb,)), ((), ())), preferred_element_type=f32)


def exchange(parts, axes):
    return lax.all_to_all(parts, axes, 0, 0, tiled=True)


def spread(row, axes, group):
    return exchange(jnp.broadcast_to(row[None], (group,) + row.shape), axes)


def ring(block, axis, distance):
    count = lax.axis_size(axis)
    return lax.ppermute(block, axis, [(i, (i + distance) % count) for i in range(count)])


def pick(stack, index):
    return lax.dynamic_index_in_dim(stack, index, 0, keepdims=False)


def together(*values):
    return lax.optimization_barrier(values)


def kernel_call(body, specs, shapes, flops, name, after=None):
    tokens = [] if after is None else [after]
    call = pl.pallas_call(
        lambda *refs: body(*refs[len(tokens) :]),
        in_specs=[pl.BlockSpec(memory_space=pl.ANY)] * len(tokens) + specs,
        out_specs=[VM] * len(shapes),
        out_shape=[jax.ShapeDtypeStruct(s, d) for s, d in shapes],
        compiler_params=pltpu.CompilerParams(vmem_limit_bytes=VMEM_LIMIT),
        cost_estimate=pl.CostEstimate(flops=flops, bytes_accessed=4 * 2**20, transcendentals=0),
        name=name,
    )
    return lambda *values: call(*tokens, *values)


def gate(value, *tokens):
    return pl.pallas_call(
        lambda *refs: None,
        in_specs=[pl.BlockSpec(memory_space=pl.ANY)] * (1 + len(tokens)),
        out_specs=pl.BlockSpec(memory_space=pl.ANY),
        out_shape=jax.ShapeDtypeStruct(value.shape, value.dtype),
        input_output_aliases={0: 0},
        cost_estimate=pl.CostEstimate(flops=LONG, bytes_accessed=2**20, transcendentals=0),
        name="gate",
    )(value, *tokens)


def slot_of_bit(strides_ref, bit):
    slot = 0
    for k in range(SLOTS - 1):
        slot = slot + jnp.where(strides_ref[k] == 1 << bit, k + 1, 0)
    return slot


def products(bits, strides_ref, x_ref, dy_ref, w1_ref, w2_ref, *send_refs):
    x, dy = x_ref[...], dy_ref[...]
    for bit, send_ref in zip(bits, send_refs):
        slot = slot_of_bit(strides_ref, bit)
        send_ref[0] = dot(x, w1_ref[slot], 1, 0).astype(bf16)
        send_ref[1] = dot(dy, w2_ref[slot], 1, 1).astype(bf16)


def sum_products(x_ref, dy_ref, w1_ref, w2_ref, *refs):
    got, total_ref = refs[:-1], refs[-1]
    own = (dot(x_ref[...], w1_ref[0], 1, 0), dot(dy_ref[...], w2_ref[0], 1, 1))
    for half in range(2):
        value = own[half]
        for ref in got:
            value = value + ref[half].astype(f32)
        total_ref[half] = value


def activations(base_ref, latent_ref, right1_ref, left2_ref, *refs):
    hd_refs, part_ref = refs[:3], refs[3]
    rank = right1_ref.shape[0]
    right1, left2 = right1_ref[...], left2_ref[...]
    z = base_ref[0] + dot(latent_ref[:, :rank], right1, 1, 0)
    g = base_ref[1] + dot(latent_ref[:, rank:], left2, 1, 1)
    cumul = 0.5 * (1.0 + lax.erf(z * root_half))
    slope = cumul + z * jnp.exp(-0.5 * z * z) * gauss_norm
    h = (z * cumul).astype(bf16)
    dz = (g * slope).astype(bf16)
    for hd_ref in hd_refs:
        hd_ref[0] = h
        hd_ref[1] = dz
    part_ref[:, :rank] = dot(h, left2, 1, 0).astype(bf16)
    part_ref[:, rank:] = dot(dz, right1, 1, 1).astype(bf16)


def block_outputs(bits, strides_ref, w1_ref, w2_ref, hd_ref, *refs):
    near, out_ref = refs[:-1], refs[-1]
    size = w1_ref.shape[1]
    block_out = dot(hd_ref[0], w2_ref[0], 1, 0)
    block_in = dot(hd_ref[1], w1_ref[0], 1, 1)
    for bit, ref in zip(bits, near):
        slot = slot_of_bit(strides_ref, bit)
        block_out = block_out + dot(ref[0], w2_ref[slot], 1, 0)
        block_in = block_in + dot(ref[1], w1_ref[slot], 1, 1)
    out_ref[:, :size] = block_out.astype(bf16)
    out_ref[:, size:] = block_in.astype(bf16)


def block_grads(bits, strides_ref, x_ref, dy_ref, latent_ref, hd_ref, *refs):
    near, out_ref = refs[:-1], refs[-1]
    size = x_ref.shape[1]
    rank = latent_ref.shape[1] // 2
    parts = out_ref.shape[0]
    rows = size // parts
    x, dy = x_ref[...], dy_ref[...]

    def store(slot, ref):
        grad1, grad2 = dot(x, ref[1], 0, 0), dot(ref[0], dy, 0, 0)
        for d in range(parts):
            own = slice(d * rows, (d + 1) * rows)
            start = pl.multiple_of(slot * rows, rows)
            out_ref[d, pl.ds(start, rows), :] = grad1[own].astype(bf16)
            start = pl.multiple_of((slot + SLOTS) * rows, rows)
            out_ref[d, pl.ds(start, rows), :] = grad2[own].astype(bf16)

    store(0, hd_ref)
    for bit, ref in zip(bits, near):
        store(slot_of_bit(strides_ref, bit), ref)
    first = 2 * SLOTS * rows
    take = rank // parts
    for d in range(parts):
        right1 = dot(latent_ref[:, d * take : (d + 1) * take], hd_ref[1], 0, 0)
        left2 = dot(latent_ref[:, rank + d * take : rank + (d + 1) * take], hd_ref[0], 0, 0)
        out_ref[d, first : first + take, :] = right1.astype(bf16)
        out_ref[d, first + take : first + 2 * take, :] = left2.astype(bf16)


def sum_grads(*refs):
    got, (first_ref, second_ref, right1_ref, left2_ref) = refs[:-4], refs[-4:]
    rows = first_ref.shape[0]
    take = right1_ref.shape[0]

    def total(low, high):
        value = got[0][low:high, :].astype(f32)
        for ref in got[1:]:
            value = value + ref[low:high, :].astype(f32)
        return value

    first_ref[...] = total(0, rows)
    second_ref[...] = total(rows, 2 * rows)
    right1_ref[...] = total(2 * rows, 2 * rows + take)
    left2_ref[...] = total(2 * rows + take, 2 * rows + 2 * take).T


def for_bits(
    bits,
    tokens,
    cotangent,
    first_blocks,
    second_blocks,
    first_left,
    first_right,
    second_left,
    second_right,
    strides,
):
    count, size = tokens.shape
    rank = first_left.shape[1]
    n_in = lax.axis_size("in")
    n_out = lax.axis_size("out")
    n_dp = lax.axis_size("dp")
    p = lax.axis_index("out")
    w1 = first_blocks[0, 0]
    w2 = second_blocks[0, 0]
    right1 = first_right[:, 0]
    left2 = second_left[0]
    share = count // n_out
    wide = 2 * rank
    tile = (wide // 128, 128)
    flops = 2 * count * size * size
    pair = ((2, count, size), bf16)

    x_share = lax.dynamic_slice_in_dim(tokens, p * share, share, 0)
    dy_share = lax.dynamic_slice_in_dim(cotangent, p * share, share, 0)
    part = jnp.concatenate([dot(x_share, first_left, 1, 0), dot(dy_share, second_right, 1, 1)], axis=1)
    got = exchange(part.astype(bf16).reshape((share,) + tile), "in")

    def sent(some, after):
        sends = kernel_call(
            partial(products, some), [SM, VM, VM, VM, VM], [pair] * len(some), LONG, "products", after
        )(strides, tokens, cotangent, w1, w2)
        return [swap_bit(send, bit) for send, bit in zip(sends, some)]

    arrived = sent([b for b in bits if b in FIRST_A], None)
    row = jnp.sum(got.astype(f32), axis=0).astype(bf16)
    arrived += sent([b for b in reversed(bits) if b not in FIRST_A], row)
    (base,) = kernel_call(
        sum_products, [VM] * (4 + len(bits)), [((2, count, size), f32)], LONG, "sum_products"
    )(tokens, cotangent, w1, w2, *arrived)
    mine = spread(row, "in", n_in)
    latent = spread(gate(mine), "out", n_out).reshape(count, wide)

    hd, first_hd, second_hd, part = kernel_call(
        activations, [VM] * 4, [pair] * 3 + [((count, wide), bf16)], 16 * flops, "activations"
    )(base, latent, right1, left2)

    got = exchange(part.reshape(n_out, share, wide), "out")
    first_hd = gate(first_hd)
    part = jnp.sum(got.astype(f32), axis=0).astype(bf16)
    second_hd = gate(second_hd, part)
    near = [swap_bit(first_hd if bit in FIRST else second_hd, bit) for bit in bits]
    got = exchange(part.reshape((share,) + tile), "in")
    row = jnp.sum(got.astype(f32), axis=0).astype(bf16)
    (blocks,) = kernel_call(
        partial(block_outputs, bits), [SM] + [VM] * (3 + len(bits)), [((count, 2 * size), bf16)], LONG, "block_outputs", row
    )(strides, w1, w2, hd, *near)

    rows = SLOTS * size // n_dp
    take = rank // n_dp
    (grads,) = kernel_call(
        partial(block_grads, bits),
        [SM] + [VM] * (4 + len(bits)),
        [((n_dp, 2 * (rows + take), size), bf16)],
        LONG,
        "block_grads",
        row,
    )(strides, tokens, cotangent, latent, hd, *near)
    mine = spread(row, "in", n_in).reshape(share, wide)
    me = lax.axis_index("dp")
    sums = [pick(grads, me)] + [ring(pick(grads, (me + d) % n_dp), "dp", d) for d in range(1, n_dp)]
    both = jnp.concatenate([mine.reshape(share * wide // 256, 256), blocks.reshape(count * 2 * size // 256, 256)])
    both = spread(gate(both, grads), "out", n_out)
    cut = share * wide // 256
    cf = both[:, :cut].reshape(count, wide)
    blocks = jnp.sum(both[:, cut:].astype(f32), axis=0).reshape(count, 2 * size)
    c, f = cf[:, :rank], cf[:, rank:]
    parts = jnp.concatenate(
        [dot(f, tokens, 0, 0).reshape(n_dp, take, size), dot(c, cotangent, 0, 0).reshape(n_dp, take, size)], axis=1
    ).astype(bf16)
    sums[0] = gate(sums[0], *sums[1:])
    parts, sums[0] = together(parts, sums[0])
    first_grad, second_grad, right1_grad, left2_grad = kernel_call(
        sum_grads,
        [VM] * n_dp,
        [((rows, size), f32), ((rows, size), f32), ((take, size), f32), ((size, take), f32)],
        LONG,
        "sum_grads",
        parts,
    )(*sums)
    parts = exchange(parts, "dp")
    output = (blocks[:, :size] + dot(c, second_right, 1, 0)).astype(bf16)
    input_grad = (blocks[:, size:] + dot(f, first_left, 1, 1)).astype(bf16)
    late = jnp.sum(parts.astype(f32), axis=0)
    left1_grad, right2_grad = late[:take].T, late[take:]
    block_shape = (1, 1, SLOTS, size // n_dp, size)
    return (
        output,
        input_grad,
        first_grad.reshape(block_shape),
        second_grad.reshape(block_shape),
        left1_grad,
        right1_grad[:, None],
        left2_grad[None],
        right2_grad,
    )


def per_device(*args):
    absent = (1 << BITS) - 1 - jnp.sum(args[-1])
    index = sum((absent >= (1 << b)).astype(jnp.int32) for b in range(1, BITS - 1))
    cases = [tuple(b for b in range(BITS) if b != gone) for gone in range(BITS - 1)]
    return lax.switch(index, [partial(for_bits, bits) for bits in cases], *args)


def solution(mesh):
    in_specs = (
        P("dp", "in"),
        P("dp", "in"),
        P("in", "out", None, None, None),
        P("in", "out", None, None, None),
        P("in", None),
        P(None, "out", "in"),
        P("out", "in", None),
        P(None, "in"),
        P(),
    )
    out_specs = (
        P("dp", "in"),
        P("dp", "in"),
        P("in", "out", None, "dp", None),
        P("in", "out", None, "dp", None),
        P("in", "dp"),
        P("dp", "out", "in"),
        P("out", "in", "dp"),
        P("dp", "in"),
    )
    return jax.shard_map(
        per_device, mesh=mesh, in_specs=in_specs, out_specs=out_specs, check_vma=False
    )
```
